32 devices in a mesh: groups: 2 (over x), gx: 16 (over z, y, core).
Axes of the slice: x: 2, y: 2, z: 4, core: 2. Of those that a mesh axis runs over, the one named last changes fastest.
Arguments:
- u_prev: float32 [256, 256, 256], P(('groups', 'gx')), parts along dimension 0, may hold values from -7 to 7
- u_cur: float32 [256, 256, 256], P(('groups', 'gx')), parts along dimension 0, may hold values from -7 to 7
- courant_sq: float32 [256, 256, 256], P(('groups', 'gx')), parts along dimension 0, may hold values from 0.1 to 0.33
- patch_map: int32 [256, 4, 256], P(('groups', 'gx')), parts along dimension 0, may hold values from 0 to 159
- absorb: float32 [320], P('groups'), parts along dimension 0, may hold values from 0.05 to 1
- checkpoint: int32 [2], P('groups'), parts along dimension 0, may hold values from 0 to 60
- target_curve: float32 [128], P('groups'), parts along dimension 0, may hold values from 0 to 2.5
- tail_energy: float32 [2], P('groups'), parts along dimension 0, may hold values from 0.5 to 4
Outputs:
- grad_prev: float32 [256, 256, 256], P(('groups', 'gx')), parts along dimension 0
- grad_cur: float32 [256, 256, 256], P(('groups', 'gx')), parts along dimension 0
- grad_absorb: float32 [320], P(('groups', 'gx')), parts along dimension 0
The draws below stay inside these ranges and needn't reach their ends.
There are 2 independent parts, one for each index of `groups`. The reference program is written for one: setup_inputs(seed, part) draws one part's arguments, and reference() takes and returns one part's arrays. A program takes and returns all parts, laid end to end along the dimension named above; each array names one. Nothing has to cross between parts.
All inputs are finite; a program needn't handle non-finite values.
Results may differ from the reference program's by a relative error of at most 0.00002.
Values sent between devices are 32-bit elements; how exact they have to be, the bound alone decides.
A program may use at most 128 MiB of HBM per device.

```python
import math
import jax
import jax.numpy as jnp
from jax import lax

CX = 8
SIDE = 256
STEPS = 4
HISTORY = 64
NX = 128
PATCHES = 160
PATCH_CELLS = 819
CELLS = 8388608


def brick_loudness(key):
    bricks = NX // CX
    phase = jax.random.randint(jax.random.fold_in(key, 5), (), 0, 2)
    strength = jax.random.uniform(jax.random.fold_in(key, 6), (bricks,), jnp.float32, 0.7, 1.0)
    parity = (jnp.arange(bricks, dtype=jnp.int32) + phase) % 2
    signed = 2.0 * parity.astype(jnp.float32) - 1.0
    loudness = jnp.exp(signed * strength)
    return jnp.repeat(loudness, CX, total_repeat_length=NX)[:, None, None]


def ramped_field(key, constant):
    subkey = jax.random.fold_in(key, constant)
    position = jnp.arange(NX, dtype=jnp.float32) / float(NX - 1)
    profile = (1.0 + 0.75 * position)[:, None, None]
    noise = jnp.clip(jax.random.normal(subkey, (NX, SIDE, SIDE), jnp.float32), -4.0, 4.0)
    return jnp.clip(noise * profile * brick_loudness(key), -7.0, 7.0)


def draw_u_prev(key, part):
    return ramped_field(key, 11)


def draw_u_cur(key, part):
    return ramped_field(key, 23)


def draw_courant_sq(key, part):
    subkey = jax.random.fold_in(key, 31)
    level = jax.random.randint(subkey, (NX, SIDE, SIDE), 0, 20)
    high = (level < 17).astype(jnp.float32)
    return 0.1 + 0.23 * high


def touch_ends(values, key, least, largest):
    dims = values.shape
    spot = [jax.random.randint(jax.random.fold_in(key, axis), (), 0, dims[axis]) for axis in range(len(dims))]
    values = values.at[tuple(spot)].set(least)
    longest = dims.index(max(dims))
    spot[longest] = (spot[longest] + 1) % dims[longest]
    return values.at[tuple(spot)].set(largest)


def setup_inputs(seed: int = 0, part: int = 0) -> dict:
    key_of = jax.random.split(jax.random.key(seed), 9)
    own_keys = jax.random.split(jax.random.fold_in(key_of[8], part), 9)
    return {
        "u_prev": draw_u_prev(jax.random.fold_in(jax.random.fold_in(key_of[8], part), 71), part),
        "u_cur": draw_u_cur(jax.random.fold_in(jax.random.fold_in(key_of[8], part), 71), part),
        "courant_sq": draw_courant_sq(jax.random.fold_in(jax.random.fold_in(key_of[8], part), 71), part),
        "patch_map": touch_ends(jax.random.randint(own_keys[3], (NX, 4, SIDE), 0, PATCHES), jax.random.fold_in(own_keys[3], 1), 0, PATCHES - 1).astype(jnp.int32),
        "absorb": jnp.clip(jnp.exp(jax.random.uniform(own_keys[4], (PATCHES,), jnp.float32, math.log(0.05), math.log(1.0))), 0.05, 1.0),
        "checkpoint": jax.random.randint(own_keys[5], (1,), 0, HISTORY - STEPS + 1).astype(jnp.int32),
        "target_curve": jnp.clip(jax.random.uniform(own_keys[6], (HISTORY,), jnp.float32, 0.0, 2.5), 0.0, 2.5),
        "tail_energy": jnp.clip(jax.random.uniform(own_keys[7], (1,), jnp.float32, 0.5, 4.0), 0.5, 4.0),
    }


def neighbours(field):
    full = jnp.pad(field, 1)
    total = full[2:, 1:-1, 1:-1] + full[:-2, 1:-1, 1:-1]
    total = total + full[1:-1, 2:, 1:-1] + full[1:-1, :-2, 1:-1]
    return total + full[1:-1, 1:-1, 2:] + full[1:-1, 1:-1, :-2]


def spread_faces(faces, side_cells):
    damping = jnp.zeros((faces.shape[0], side_cells, side_cells), jnp.float32)
    damping = damping.at[:, 0, :].add(faces[:, 0])
    damping = damping.at[:, -1, :].add(faces[:, 1])
    damping = damping.at[:, :, 0].add(faces[:, 2])
    return damping.at[:, :, -1].add(faces[:, 3])


def collect_faces(field):
    return jnp.stack([field[:, 0, :], field[:, -1, :], field[:, :, 0], field[:, :, -1]], axis=1)


def reference(u_prev, u_cur, courant_sq, patch_map, absorb, checkpoint, target_curve, tail_energy):
    damping = spread_faces(absorb[patch_map], SIDE)
    states = [u_prev, u_cur]
    for turn_index in range(STEPS):
        prior, now = states[-2], states[-1]
        states.append((2.0 * now - (1.0 - damping) * prior + courant_sq * (neighbours(now) - 6.0 * now)) / (1.0 + damping))
    energy = jnp.stack([jnp.sum(field * field) for field in states[2:]]) / float(CELLS)
    targets = lax.dynamic_slice_in_dim(target_curve, checkpoint[0], STEPS)
    schroeder = tail_energy[0] + jnp.cumsum(energy[::-1])[::-1]
    slopes = 2.0 * (jnp.log(schroeder) - targets) / schroeder
    weights = jnp.cumsum(slopes)
    inverse_gain = 1.0 / (1.0 + damping)
    retain = 1.0 - damping
    adjoint = 2.0 * weights[STEPS - 1] * states[STEPS + 1]
    w_later = jnp.zeros_like(u_cur)
    grad_damp = jnp.zeros_like(u_cur)
    for back_index in range(STEPS, 0, -1):
        weighted = inverse_gain * adjoint
        grad_damp = grad_damp + weighted * (states[back_index - 1] - states[back_index + 1])
        product = courant_sq * weighted
        fresh = 2.0 * weighted + neighbours(product) - 6.0 * product - retain * w_later
        if back_index > 1:
            fresh = fresh + 2.0 * weights[back_index - 2] * states[back_index]
        w_later = weighted
        adjoint = fresh
    grad_prev = -retain * w_later
    summed = jax.ops.segment_sum(collect_faces(grad_damp).reshape(-1), patch_map.reshape(-1), PATCHES)
    return grad_prev, adjoint, summed / float(PATCH_CELLS)
```

```python
import functools

import jax
import jax.numpy as jnp
from jax import lax
from jax.experimental import pallas as pl
from jax.experimental.pallas import tpu as pltpu
from jax.sharding import PartitionSpec as P

STEPS = 4
PATCH_CELLS = 819
PAD = 8
ROWS = 32
MESH = pl.DeviceIdType.MESH


def kernel(
    n, all_cells,
    prev_hbm, cur_hbm, courant_hbm, map_ref, absorb_ref, check_ref, target_ref, tail_ref,
    gprev_hbm, gcur_hbm, gabs_ref,
    u, p, last, prev, cs, damp, inv, w, gprev, gcur,
    map_t, faces, energy, emsg, eslots, gains, part, pslots,
    local_sem, send_sem, recv_sem, esend, erecv, psend, precv,
):
    me = lax.axis_index("gx")
    depth, side = prev.shape[0], prev.shape[1]
    chunks = side // ROWS
    patches = absorb_ref.shape[0]
    owned = patches // n
    inner = pl.ds(PAD, side)
    has_left, has_right = me > 0, me < n - 1

    loads = [
        pltpu.make_async_copy(cur_hbm, u.at[0, pl.ds(1, depth), inner, :], local_sem.at[0]),
        pltpu.make_async_copy(prev_hbm, prev, local_sem.at[1]),
        pltpu.make_async_copy(courant_hbm, cs, local_sem.at[2]),
    ]
    for copy in loads:
        copy.start()

    border = jnp.zeros((PAD, side), jnp.float32)
    for field in (u, p):
        for k in range(STEPS):
            def clear(x, carry, field=field, k=k):
                field[k, x, 0:PAD, :] = border
                field[k, x, PAD + side : PAD + side + PAD, :] = border
                return carry

            lax.fori_loop(0, depth + 2, clear, 0)

    def clear_halo(layer):
        for field in (u, p):
            for k in range(STEPS):
                field[k, layer, PAD : PAD + side, :] = jnp.zeros((side, side), jnp.float32)

    @pl.when(me == 0)
    def _():
        clear_halo(0)

    @pl.when(me == n - 1)
    def _():
        clear_halo(depth + 1)

    barrier = pltpu.get_barrier_semaphore()

    def greet(d, carry):
        pl.semaphore_signal(
            barrier, inc=1, device_id={"gx": lax.rem(me + d, n)}, device_id_type=MESH
        )
        return carry

    lax.fori_loop(1, n, greet, 0)
    pl.semaphore_wait(barrier, n - 1)

    def exchange(e):
        field, k = (u, e) if e < STEPS else (p, e - STEPS)
        low = cur_hbm.at[0] if e == 0 else field.at[k, 1, inner, :]
        high = cur_hbm.at[depth - 1] if e == 0 else field.at[k, depth, inner, :]
        to_left = pltpu.make_async_remote_copy(
            src_ref=low, dst_ref=field.at[k, depth + 1, inner, :],
            send_sem=send_sem.at[e, 0], recv_sem=recv_sem.at[e, 0],
            device_id={"gx": jnp.maximum(me - 1, 0)}, device_id_type=MESH,
        )
        to_right = pltpu.make_async_remote_copy(
            src_ref=high, dst_ref=field.at[k, 0, inner, :],
            send_sem=send_sem.at[e, 1], recv_sem=recv_sem.at[e, 1],
            device_id={"gx": jnp.minimum(me + 1, n - 1)}, device_id_type=MESH,
        )
        return to_left, to_right

    def send(e):
        to_left, to_right = exchange(e)
        pl.when(has_left)(to_left.start)
        pl.when(has_right)(to_right.start)

    def receive(e):
        to_left, to_right = exchange(e)
        pl.when(has_right)(to_left.wait_recv)
        pl.when(has_left)(to_right.wait_recv)

    def sent(e):
        to_left, to_right = exchange(e)
        pl.when(has_left)(to_left.wait_send)
        pl.when(has_right)(to_right.wait_send)

    send(0)

    lane = lax.broadcasted_iota(jnp.int32, (ROWS, side), 1)
    row = lax.broadcasted_iota(jnp.int32, (ROWS, side), 0)

    for x in range(depth):
        for f in range(4):
            map_t[f, x : x + 1, :] = map_ref[x, f : f + 1, :]
    maps = [map_t[f] for f in range(4)]

    def look_up(i, found):
        value = absorb_ref[i]
        return tuple(jnp.where(m == i, value, s) for m, s in zip(maps, found))

    found = lax.fori_loop(
        0, patches, look_up, tuple(jnp.zeros((depth, side), jnp.float32) for _ in range(4)),
        unroll=4,
    )
    for f in range(4):
        faces[f] = found[f]

    def spread(i, carry):
        x, r = i // chunks, (i % chunks) * ROWS
        r = pl.multiple_of(r, ROWS)
        at = row + r
        f0, f1, f2, f3 = (faces[f, pl.ds(x, 1), :] for f in range(4))
        diagonal = lane == at
        c2 = jnp.sum(jnp.where(diagonal, f2, 0.0), axis=1, keepdims=True)
        c3 = jnp.sum(jnp.where(diagonal, f3, 0.0), axis=1, keepdims=True)
        s = jnp.where(at == 0, f0, 0.0) + jnp.where(at == side - 1, f1, 0.0)
        s = s + jnp.where(lane == 0, c2, 0.0) + jnp.where(lane == side - 1, c3, 0.0)
        damp[x, pl.ds(r, ROWS), :] = s
        inv[x, pl.ds(r, ROWS), :] = 1.0 / (1.0 + s)
        return carry

    lax.fori_loop(0, depth * chunks, spread, 0)
    for copy in loads:
        copy.wait()

    def around(field, k, x, r):
        tall = field[k, x + 1, pl.ds(r, ROWS + 2 * PAD), :]
        mid = tall[PAD : PAD + ROWS]
        here = pl.ds(r + PAD, ROWS)
        total = field[k, x, here, :] + field[k, x + 2, here, :]
        total = total + tall[PAD - 1 : PAD - 1 + ROWS] + tall[PAD + 1 : PAD + 1 + ROWS]
        total = total + jnp.where(lane == 0, 0.0, pltpu.roll(mid, 1, 1))
        total = total + jnp.where(lane == side - 1, 0.0, pltpu.roll(mid, side - 1, 1))
        return mid, total

    def over(planes, body, init):
        ends = planes == "ends"
        count = 2 if ends else depth - 2

        def step(i, carry):
            layer = i // chunks
            x = layer * (depth - 1) if ends else layer + 1
            return body(x, pl.multiple_of((i % chunks) * ROWS, ROWS), carry)

        return lax.fori_loop(0, count * chunks, step, init)

    def forward(k):
        def body(x, r, acc):
            at = pl.ds(r, ROWS)
            here = pl.ds(r + PAD, ROWS)
            mid, total = around(u, k, x, r)
            prior = prev[x, at, :] if k == 0 else u[k - 1, x + 1, here, :]
            c = cs[x, at, :]
            scale = inv[x, at, :]
            new = (2.0 * mid - (1.0 - damp[x, at, :]) * prior + c * (total - 6.0 * mid)) * scale
            if k < STEPS - 1:
                u[k + 1, x + 1, here, :] = new
            else:
                last[x, at, :] = new
                weighted = scale * new
                w[STEPS - 1, x, at, :] = weighted
                p[0, x + 1, here, :] = c * weighted
            square = new * new
            for b in range(0, ROWS, 8):
                acc = acc + square[b : b + 8]
            return acc

        return body

    nothing = jnp.zeros((8, side), jnp.float32)
    for k in range(STEPS):
        receive(k)
        acc = over("ends", forward(k), nothing)
        send(k + 1)
        energy[k] = over("middle", forward(k), acc)

    emsg[...] = jnp.zeros_like(emsg)
    for k in range(STEPS):
        line = jnp.sum(energy[k], axis=0, keepdims=True)
        half = line[:, :128]
        for b in range(128, side, 128):
            half = half + line[:, b : b + 128]
        emsg[k : k + 1, :] = half

    def e_copy(d):
        return pltpu.make_async_remote_copy(
            src_ref=emsg, dst_ref=eslots.at[d], send_sem=esend.at[d], recv_sem=erecv.at[d],
            device_id={"gx": lax.rem(me + d, n)}, device_id_type=MESH,
        )

    def p_copy(d):
        to = lax.rem(me + d, n)
        return pltpu.make_async_remote_copy(
            src_ref=part.at[to], dst_ref=pslots.at[d], send_sem=psend.at[d], recv_sem=precv.at[d],
            device_id={"gx": to}, device_id_type=MESH,
        )

    def each(action):
        def step(d, carry):
            action(d)
            return carry

        lax.fori_loop(1, n, step, 0)

    each(lambda d: e_copy(d).start())
    each(lambda d: e_copy(d).wait_recv())
    summed = lax.fori_loop(1, n, lambda d, t: t + eslots[d], emsg[...])
    summed = jnp.sum(summed, axis=1, keepdims=True) / all_cells
    tail, start = tail_ref[0], check_ref[0]
    later = jnp.zeros((1, side), jnp.float32) + tail
    slopes = [None] * STEPS
    for k in range(STEPS - 1, -1, -1):
        later = later + summed[k : k + 1, :]
        slopes[k] = 2.0 * (jnp.log(later) - target_ref[start + k]) / later
    running = jnp.zeros((1, side), jnp.float32)
    for k in range(STEPS):
        running = running + slopes[k]
        gains[k : k + 1, :] = 2.0 * running

    def backward(j):
        slot = STEPS - j

        def body(x, r, carry):
            at = pl.ds(r, ROWS)
            here = pl.ds(r + PAD, ROWS)
            mid, total = around(p, slot, x, r)
            fresh = 2.0 * w[j - 1, x, at, :] + total - 6.0 * mid
            if j == STEPS:
                fresh = fresh * gains[STEPS - 1 : STEPS, :]
            else:
                after = w[j, x, at, :]
                if j == STEPS - 1:
                    after = after * gains[STEPS - 1 : STEPS, :]
                fresh = fresh - (1.0 - damp[x, at, :]) * after
            if j == 1:
                gcur[x, at, :] = fresh
                return carry
            fresh = fresh + gains[j - 2 : j - 1, :] * u[j - 1, x + 1, here, :]
            weighted = inv[x, at, :] * fresh
            w[j - 2, x, at, :] = weighted
            p[slot + 1, x + 1, here, :] = cs[x, at, :] * weighted
            if j == 2:
                gprev[x, at, :] = (damp[x, at, :] - 1.0) * weighted
            return carry

        return body

    for j in range(STEPS, 1, -1):
        receive(2 * STEPS - j)
        over("ends", backward(j), 0)
        send(2 * STEPS - j + 1)
        over("middle", backward(j), 0)

    out_prev = pltpu.make_async_copy(gprev, gprev_hbm, local_sem.at[3])
    out_prev.start()

    def state(k, x, at, cells):
        if k < 0:
            return prev[x, at, cells]
        if k == STEPS:
            return last[x, at, cells]
        return u[k, x + 1, pl.ds(at.start + PAD, at.size), cells]

    def product(x, at, cells):
        total = None
        for j in range(STEPS, 0, -1):
            term = w[j - 1, x, at, cells] * (state(j - 2, x, at, cells) - state(j, x, at, cells))
            if j == STEPS:
                term = term * gains[STEPS - 1 : STEPS, cells]
            total = term if total is None else total + term
        return total

    def collect(x, carry):
        top = product(x, pl.ds(0, 8), slice(0, side))
        bottom = product(x, pl.ds(side - 8, 8), slice(0, side))
        faces[0, pl.ds(x, 1), :] = top[0:1]
        faces[1, pl.ds(x, 1), :] = bottom[7:8]

        def column(i, lines):
            r = pl.multiple_of(i * ROWS, ROWS)
            diagonal = lane == row + r
            at = pl.ds(r, ROWS)
            left = product(x, at, slice(0, 128))[:, 0:1]
            right = product(x, at, slice(side - 128, side))[:, 127:128]
            return tuple(
                line + jnp.sum(jnp.where(diagonal, c, 0.0), axis=0, keepdims=True)
                for line, c in zip(lines, (left, right))
            )

        blank = jnp.zeros((1, side), jnp.float32)
        lines = lax.fori_loop(0, chunks, column, (blank, blank))
        faces[2, pl.ds(x, 1), :] = lines[0]
        faces[3, pl.ds(x, 1), :] = lines[1]
        return carry

    lax.fori_loop(0, depth, collect, 0)
    place = lax.broadcasted_iota(jnp.int32, (8, 128), 1)

    def by_owner(i, carry):
        tile = jnp.zeros((8, 128), jnp.float32)
        for k in range(owned):
            hit = None
            for f in range(4):
                term = jnp.where(map_t[f] == i * owned + k, faces[f], 0.0)
                hit = term if hit is None else hit + term
            line = jnp.sum(hit, axis=0, keepdims=True)
            whole = jnp.sum(line, axis=1, keepdims=True)
            tile = jnp.where(place == k, whole, tile)
        part[i] = tile
        return carry

    lax.fori_loop(0, n, by_owner, 0)
    each(lambda d: p_copy(d).start())

    over("middle", backward(1), 0)
    ends = depth - 2
    out_mid = pltpu.make_async_copy(
        gcur.at[pl.ds(1, ends)], gcur_hbm.at[pl.ds(1, ends)], local_sem.at[4]
    )
    out_mid.start()
    receive(2 * STEPS - 1)
    over("ends", backward(1), 0)
    out_low = pltpu.make_async_copy(gcur.at[0], gcur_hbm.at[0], local_sem.at[5])
    out_high = pltpu.make_async_copy(gcur.at[depth - 1], gcur_hbm.at[depth - 1], local_sem.at[6])
    out_low.start()
    out_high.start()

    each(lambda d: p_copy(d).wait_recv())
    mine = lax.fori_loop(1, n, lambda d, t: t + pslots[d], part[me])
    gabs_ref[...] = mine / float(PATCH_CELLS)

    for e in range(2 * STEPS):
        sent(e)
    each(lambda d: e_copy(d).wait_send())
    each(lambda d: p_copy(d).wait_send())
    for copy in (out_prev, out_mid, out_low, out_high):
        copy.wait()


def on_device(n, u_prev, u_cur, courant_sq, patch_map, absorb, checkpoint, target_curve, tail_energy):
    depth, side = u_cur.shape[0], u_cur.shape[1]
    f32 = jnp.float32
    brick = pltpu.VMEM((depth, side, side), f32)
    padded = pltpu.VMEM((STEPS, depth + 2, side + 2 * PAD, side), f32)
    hbm = pl.BlockSpec(memory_space=pl.ANY)
    vmem = pl.BlockSpec(memory_space=pltpu.VMEM)
    smem = pl.BlockSpec(memory_space=pltpu.SMEM)
    dma = pltpu.SemaphoreType.DMA
    grad_prev, grad_cur, tile = pl.pallas_call(
        functools.partial(kernel, n, float(depth * n * side * side)),
        out_shape=(
            jax.ShapeDtypeStruct(u_cur.shape, f32),
            jax.ShapeDtypeStruct(u_cur.shape, f32),
            jax.ShapeDtypeStruct((8, 128), f32),
        ),
        in_specs=[hbm, hbm, hbm, vmem, smem, smem, smem, smem],
        out_specs=(hbm, hbm, vmem),
        scratch_shapes=[
            padded, padded, brick, brick, brick, brick, brick,
            pltpu.VMEM((STEPS, depth, side, side), f32), brick, brick,
            pltpu.VMEM((4, depth, side), jnp.int32),
            pltpu.VMEM((4, depth, side), f32),
            pltpu.VMEM((STEPS, 8, side), f32),
            pltpu.VMEM((8, 128), f32),
            pltpu.VMEM((n, 8, 128), f32),
            pltpu.VMEM((8, side), f32),
            pltpu.VMEM((n, 8, 128), f32),
            pltpu.VMEM((n, 8, 128), f32),
            dma((7,)), dma((2 * STEPS, 2)), dma((2 * STEPS, 2)),
            dma((n,)), dma((n,)), dma((n,)), dma((n,)),
        ],
        compiler_params=pltpu.CompilerParams(
            collective_id=0, has_side_effects=True, vmem_limit_bytes=56 * 1024 * 1024
        ),
    )(u_prev, u_cur, courant_sq, patch_map, absorb, checkpoint, target_curve, tail_energy)
    return grad_prev, grad_cur, tile[0, : absorb.shape[0] // n]


def solution(mesh):
    field = P(("groups", "gx"), None, None)
    return jax.shard_map(
        functools.partial(on_device, mesh.shape["gx"]),
        mesh=mesh,
        in_specs=(field, field, field, field, P("groups"), P("groups"), P("groups"), P("groups")),
        out_specs=(field, field, P(("groups", "gx"))),
        check_vma=False,
    )
```

```python
import functools

import jax
import jax.numpy as jnp
from jax import lax
from jax.experimental import pallas as pl
from jax.experimental.pallas import tpu as pltpu
from jax.sharding import PartitionSpec as P

STEPS = 4
PATCH_CELLS = 819
PAD = 8
ROWS = 32
BLOCKS = 2
MESH = pl.DeviceIdType.MESH


def kernel(
    n, all_cells,
    prev_hbm, cur_hbm, courant_hbm, map_ref, absorb_ref, check_ref, target_ref, tail_ref,
    gprev_hbm, gcur_hbm, gabs_ref,
    u, p, last, prev, cs, damp, inv, w, gprev, gcur,
    map_t, faces, energy, emsg, eslots, gains, part, pslots,
    local_sem, send_sem, recv_sem, esend, erecv, psend, precv,
):
    me = lax.axis_index("gx")
    depth, side = prev.shape[0], prev.shape[1]
    patches = absorb_ref.shape[0]
    owned = patches // n
    inner = pl.ds(PAD, side)
    has_left, has_right = me > 0, me < n - 1

    loads = [
        pltpu.make_async_copy(cur_hbm, u.at[0, pl.ds(1, depth), inner, :], local_sem.at[0]),
        pltpu.make_async_copy(prev_hbm, prev, local_sem.at[1]),
        pltpu.make_async_copy(courant_hbm, cs, local_sem.at[2]),
    ]
    for copy in loads:
        copy.start()

    border = jnp.zeros((PAD, side), jnp.float32)
    for field in (u, p):
        for k in range(STEPS):
            def clear(x, carry, field=field, k=k):
                field[k, x, 0:PAD, :] = border
                field[k, x, PAD + side : PAD + side + PAD, :] = border
                return carry

            lax.fori_loop(0, depth + 2, clear, 0)

    def clear_halo(layer):
        for field in (u, p):
            for k in range(STEPS):
                field[k, layer, PAD : PAD + side, :] = jnp.zeros((side, side), jnp.float32)

    @pl.when(me == 0)
    def _():
        clear_halo(0)

    @pl.when(me == n - 1)
    def _():
        clear_halo(depth + 1)

    barrier = pltpu.get_barrier_semaphore()

    def greet(d, carry):
        pl.semaphore_signal(
            barrier, inc=1, device_id={"gx": lax.rem(me + d, n)}, device_id_type=MESH
        )
        return carry

    lax.fori_loop(1, n, greet, 0)
    pl.semaphore_wait(barrier, n - 1)

    span = side // BLOCKS

    def exchange(e, to_right, b):
        field, k = (u, e) if e < STEPS else (p, e - STEPS)
        rows = pl.ds(PAD + b * span, span)
        layer, landing = (depth, 0) if to_right else (1, depth + 1)
        way = 1 if to_right else 0
        to = jnp.minimum(me + 1, n - 1) if to_right else jnp.maximum(me - 1, 0)
        source = field.at[k, layer, rows, :]
        if e == 0:
            source = cur_hbm.at[layer - 1, pl.ds(b * span, span), :]
        return pltpu.make_async_remote_copy(
            src_ref=source, dst_ref=field.at[k, landing, rows, :],
            send_sem=send_sem.at[e, way, b], recv_sem=recv_sem.at[e, way, b],
            device_id={"gx": to}, device_id_type=MESH,
        )

    def send(e, to_right, b):
        @pl.when(has_right if to_right else has_left)
        def _():
            exchange(e, to_right, b).start()

    def receive(e, from_left, b):
        @pl.when(has_left if from_left else has_right)
        def _():
            exchange(e, from_left, b).wait_recv()

    def sent(e):
        for to_right, there in ((False, has_left), (True, has_right)):
            @pl.when(there)
            def _(to_right=to_right):
                for b in range(BLOCKS):
                    exchange(e, to_right, b).wait_send()

    for b in range(BLOCKS):
        send(0, False, b)
        send(0, True, b)

    lane = lax.broadcasted_iota(jnp.int32, (ROWS, side), 1)
    row = lax.broadcasted_iota(jnp.int32, (ROWS, side), 0)

    for x in range(depth):
        for f in range(4):
            map_t[f, x : x + 1, :] = map_ref[x, f : f + 1, :]
    maps = [map_t[f] for f in range(4)]

    def look_up(i, found):
        value = absorb_ref[i]
        return tuple(jnp.where(m == i, value, s) for m, s in zip(maps, found))

    found = lax.fori_loop(
        0, patches, look_up, tuple(jnp.zeros((depth, side), jnp.float32) for _ in range(4)),
        unroll=4,
    )
    for f in range(4):
        faces[f] = found[f]

    def spread(x, carry):
        f0, f1, f2, f3 = (faces[f, pl.ds(x, 1), :] for f in range(4))
        for r in range(0, side, ROWS):
            diagonal = lane == row + r
            c2 = jnp.sum(jnp.where(diagonal, f2, 0.0), axis=1, keepdims=True)
            c3 = jnp.sum(jnp.where(diagonal, f3, 0.0), axis=1, keepdims=True)
            s = jnp.where(lane == 0, c2, 0.0) + jnp.where(lane == side - 1, c3, 0.0)
            if r == 0:
                s = s + jnp.where(row == 0, f0, 0.0)
            if r == side - ROWS:
                s = s + jnp.where(row == ROWS - 1, f1, 0.0)
            damp[x, r : r + ROWS, :] = s
            inv[x, r : r + ROWS, :] = 1.0 / (1.0 + s)
        return carry

    lax.fori_loop(0, depth, spread, 0)
    for copy in loads:
        copy.wait()

    def around(field, k, x, r):
        tall = field[k, x + 1, pl.ds(r, ROWS + 2 * PAD), :]
        mid = tall[PAD : PAD + ROWS]
        here = pl.ds(r + PAD, ROWS)
        total = field[k, x, here, :] + field[k, x + 2, here, :]
        total = total + tall[PAD - 1 : PAD - 1 + ROWS] + tall[PAD + 1 : PAD + 1 + ROWS]
        total = total + jnp.where(lane == 0, 0.0, pltpu.roll(mid, 1, 1))
        total = total + jnp.where(lane == side - 1, 0.0, pltpu.roll(mid, side - 1, 1))
        return mid, total

    def middle(body, carry):
        def step(x, carry):
            for r in range(0, side, ROWS):
                carry = body(x, r, carry)
            return carry

        return lax.fori_loop(1, depth - 1, step, carry)

    def outer(e, body, carry, last_one=False):
        for b in range(BLOCKS):
            for x, is_right in ((0, False), (depth - 1, True)):
                receive(e, not is_right, b)
                for r in range(b * span, (b + 1) * span, ROWS):
                    carry = body(x, r, carry)
                if not last_one:
                    send(e + 1, is_right, b)
        return carry

    def forward(k):
        def body(x, r, acc):
            at = pl.ds(r, ROWS)
            here = pl.ds(r + PAD, ROWS)
            mid, total = around(u, k, x, r)
            prior = prev[x, at, :] if k == 0 else u[k - 1, x + 1, here, :]
            c = cs[x, at, :]
            scale = inv[x, at, :]
            new = (2.0 * mid - (1.0 - damp[x, at, :]) * prior + c * (total - 6.0 * mid)) * scale
            if k < STEPS - 1:
                u[k + 1, x + 1, here, :] = new
            else:
                last[x, at, :] = new
                weighted = scale * new
                w[STEPS - 1, x, at, :] = weighted
                p[0, x + 1, here, :] = c * weighted
            square = new * new
            for b in range(0, ROWS, 8):
                acc = acc + square[b : b + 8]
            return acc

        return body

    nothing = jnp.zeros((8, side), jnp.float32)
    for k in range(STEPS):
        acc = outer(k, forward(k), nothing)
        energy[k] = middle(forward(k), acc)

    emsg[...] = jnp.zeros_like(emsg)
    for k in range(STEPS):
        line = jnp.sum(energy[k], axis=0, keepdims=True)
        half = line[:, :128]
        for b in range(128, side, 128):
            half = half + line[:, b : b + 128]
        emsg[k : k + 1, :] = half

    def e_copy(d):
        return pltpu.make_async_remote_copy(
            src_ref=emsg, dst_ref=eslots.at[d], send_sem=esend.at[d], recv_sem=erecv.at[d],
            device_id={"gx": lax.rem(me + d, n)}, device_id_type=MESH,
        )

    def p_copy(d):
        to = lax.rem(me + d, n)
        return pltpu.make_async_remote_copy(
            src_ref=part.at[to], dst_ref=pslots.at[d], send_sem=psend.at[d], recv_sem=precv.at[d],
            device_id={"gx": to}, device_id_type=MESH,
        )

    def each(action):
        def step(d, carry):
            action(d)
            return carry

        lax.fori_loop(1, n, step, 0)

    each(lambda d: e_copy(d).start())
    each(lambda d: e_copy(d).wait_recv())
    summed = lax.fori_loop(1, n, lambda d, t: t + eslots[d], emsg[...])
    summed = jnp.sum(summed, axis=1, keepdims=True) / all_cells
    tail, start = tail_ref[0], check_ref[0]
    later = jnp.zeros((1, side), jnp.float32) + tail
    slopes = [None] * STEPS
    for k in range(STEPS - 1, -1, -1):
        later = later + summed[k : k + 1, :]
        slopes[k] = 2.0 * (jnp.log(later) - target_ref[start + k]) / later
    running = jnp.zeros((1, side), jnp.float32)
    for k in range(STEPS):
        running = running + slopes[k]
        gains[k : k + 1, :] = 2.0 * running

    def backward(j):
        slot = STEPS - j

        def body(x, r, carry):
            at = pl.ds(r, ROWS)
            here = pl.ds(r + PAD, ROWS)
            mid, total = around(p, slot, x, r)
            fresh = 2.0 * w[j - 1, x, at, :] + total - 6.0 * mid
            if j == STEPS:
                fresh = fresh * gains[STEPS - 1 : STEPS, :]
            else:
                after = w[j, x, at, :]
                if j == STEPS - 1:
                    after = after * gains[STEPS - 1 : STEPS, :]
                fresh = fresh - (1.0 - damp[x, at, :]) * after
            if j == 1:
                gcur[x, at, :] = fresh
                return carry
            fresh = fresh + gains[j - 2 : j - 1, :] * u[j - 1, x + 1, here, :]
            weighted = inv[x, at, :] * fresh
            w[j - 2, x, at, :] = weighted
            p[slot + 1, x + 1, here, :] = cs[x, at, :] * weighted
            if j == 2:
                gprev[x, at, :] = (damp[x, at, :] - 1.0) * weighted
            return carry

        return body

    for j in range(STEPS, 1, -1):
        outer(2 * STEPS - j, backward(j), 0)
        middle(backward(j), 0)

    out_prev = pltpu.make_async_copy(gprev, gprev_hbm, local_sem.at[3])
    out_prev.start()

    def state(k, x, at, cells):
        if k < 0:
            return prev[x, at, cells]
        if k == STEPS:
            return last[x, at, cells]
        return u[k, x + 1, pl.ds(at.start + PAD, at.size), cells]

    def product(x, at, cells):
        total = None
        for j in range(STEPS, 0, -1):
            term = w[j - 1, x, at, cells] * (state(j - 2, x, at, cells) - state(j, x, at, cells))
            if j == STEPS:
                term = term * gains[STEPS - 1 : STEPS, cells]
            total = term if total is None else total + term
        return total

    def collect(x, carry):
        top = product(x, pl.ds(0, 8), slice(0, side))
        bottom = product(x, pl.ds(side - 8, 8), slice(0, side))
        faces[0, pl.ds(x, 1), :] = top[0:1]
        faces[1, pl.ds(x, 1), :] = bottom[7:8]

        lines = [jnp.zeros((1, side), jnp.float32)] * 2
        for r in range(0, side, ROWS):
            diagonal = lane == row + r
            at = pl.ds(r, ROWS)
            left = product(x, at, slice(0, 128))[:, 0:1]
            right = product(x, at, slice(side - 128, side))[:, 127:128]
            lines = [
                line + jnp.sum(jnp.where(diagonal, c, 0.0), axis=0, keepdims=True)
                for line, c in zip(lines, (left, right))
            ]
        faces[2, pl.ds(x, 1), :] = lines[0]
        faces[3, pl.ds(x, 1), :] = lines[1]
        return carry

    lax.fori_loop(0, depth, collect, 0)
    place = lax.broadcasted_iota(jnp.int32, (8, 128), 1)

    walls = [faces[f] for f in range(4)]

    def by_owner(i, carry):
        tile = jnp.zeros((8, 128), jnp.float32)
        for k in range(owned):
            hit = None
            for f in range(4):
                term = jnp.where(maps[f] == i * owned + k, walls[f], 0.0)
                hit = term if hit is None else hit + term
            line = jnp.sum(hit, axis=0, keepdims=True)
            whole = jnp.sum(line, axis=1, keepdims=True)
            tile = jnp.where(place == k, whole, tile)
        part[i] = tile
        return carry

    lax.fori_loop(0, n, by_owner, 0)
    each(lambda d: p_copy(d).start())

    middle(backward(1), 0)
    ends = depth - 2
    out_mid = pltpu.make_async_copy(
        gcur.at[pl.ds(1, ends)], gcur_hbm.at[pl.ds(1, ends)], local_sem.at[4]
    )
    out_mid.start()
    outer(2 * STEPS - 1, backward(1), 0, last_one=True)
    out_low = pltpu.make_async_copy(gcur.at[0], gcur_hbm.at[0], local_sem.at[5])
    out_high = pltpu.make_async_copy(gcur.at[depth - 1], gcur_hbm.at[depth - 1], local_sem.at[6])
    out_low.start()
    out_high.start()

    each(lambda d: p_copy(d).wait_recv())
    mine = lax.fori_loop(1, n, lambda d, t: t + pslots[d], part[me])
    gabs_ref[...] = mine / float(PATCH_CELLS)

    for e in range(2 * STEPS):
        sent(e)
    each(lambda d: e_copy(d).wait_send())
    each(lambda d: p_copy(d).wait_send())
    for copy in (out_prev, out_mid, out_low, out_high):
        copy.wait()


def on_device(n, u_prev, u_cur, courant_sq, patch_map, absorb, checkpoint, target_curve, tail_energy):
    depth, side = u_cur.shape[0], u_cur.shape[1]
    f32 = jnp.float32
    brick = pltpu.VMEM((depth, side, side), f32)
    padded = pltpu.VMEM((STEPS, depth + 2, side + 2 * PAD, side), f32)
    hbm = pl.BlockSpec(memory_space=pl.ANY)
    vmem = pl.BlockSpec(memory_space=pltpu.VMEM)
    smem = pl.BlockSpec(memory_space=pltpu.SMEM)
    dma = pltpu.SemaphoreType.DMA
    grad_prev, grad_cur, tile = pl.pallas_call(
        functools.partial(kernel, n, float(depth * n * side * side)),
        out_shape=(
            jax.ShapeDtypeStruct(u_cur.shape, f32),
            jax.ShapeDtypeStruct(u_cur.shape, f32),
            jax.ShapeDtypeStruct((8, 128), f32),
        ),
        in_specs=[hbm, hbm, hbm, vmem, smem, smem, smem, smem],
        out_specs=(hbm, hbm, vmem),
        scratch_shapes=[
            padded, padded, brick, brick, brick, brick, brick,
            pltpu.VMEM((STEPS, depth, side, side), f32), brick, brick,
            pltpu.VMEM((4, depth, side), jnp.int32),
            pltpu.VMEM((4, depth, side), f32),
            pltpu.VMEM((STEPS, 8, side), f32),
            pltpu.VMEM((8, 128), f32),
            pltpu.VMEM((n, 8, 128), f32),
            pltpu.VMEM((8, side), f32),
            pltpu.VMEM((n, 8, 128), f32),
            pltpu.VMEM((n, 8, 128), f32),
            dma((7,)), dma((2 * STEPS, 2, BLOCKS)), dma((2 * STEPS, 2, BLOCKS)),
            dma((n,)), dma((n,)), dma((n,)), dma((n,)),
        ],
        compiler_params=pltpu.CompilerParams(
            collective_id=0, has_side_effects=True, vmem_limit_bytes=56 * 1024 * 1024
        ),
    )(u_prev, u_cur, courant_sq, patch_map, absorb, checkpoint, target_curve, tail_energy)
    return grad_prev, grad_cur, tile[0, : absorb.shape[0] // n]


def solution(mesh):
    field = P(("groups", "gx"), None, None)
    return jax.shard_map(
        functools.partial(on_device, mesh.shape["gx"]),
        mesh=mesh,
        in_specs=(field, field, field, field, P("groups"), P("groups"), P("groups"), P("groups")),
        out_specs=(field, field, P(("groups", "gx"))),
        check_vma=False,
    )
```

```python
import functools

import jax
import jax.numpy as jnp
from jax import lax
from jax.experimental import pallas as pl
from jax.experimental.pallas import tpu as pltpu
from jax.sharding import PartitionSpec as P

STEPS = 4
PATCH_CELLS = 819
PAD = 8
ROWS = 32
BLOCKS = 2
MESH = pl.DeviceIdType.MESH


def kernel(
    n, all_cells,
    prev_hbm, cur_hbm, courant_hbm, map_ref, absorb_ref, check_ref, target_ref, tail_ref,
    gprev, gcur, gabs_ref,
    u, p, last, prev, cs, damp, inv, w,
    map_t, faces, energy, emsg, eslots, gains, part, pslots,
    local_sem, send_sem, recv_sem, esend, erecv, psend, precv,
):
    me = lax.axis_index("gx")
    depth, side = prev.shape[0], prev.shape[1]
    patches = absorb_ref.shape[0]
    owned = patches // n
    inner = pl.ds(PAD, side)
    has_left, has_right = me > 0, me < n - 1

    loads = [
        pltpu.make_async_copy(cur_hbm, u.at[0, pl.ds(1, depth), inner, :], local_sem.at[0]),
        pltpu.make_async_copy(prev_hbm, prev, local_sem.at[1]),
        pltpu.make_async_copy(courant_hbm, cs, local_sem.at[2]),
    ]
    for copy in loads:
        copy.start()

    barrier = pltpu.get_barrier_semaphore()

    def greet(d, carry):
        pl.semaphore_signal(
            barrier, inc=1, device_id={"gx": lax.rem(me + d, n)}, device_id_type=MESH
        )
        return carry

    lax.fori_loop(1, n, greet, 0)
    pl.semaphore_wait(barrier, n - 1)

    span = side // BLOCKS

    def exchange(e, to_right, b):
        field, k = (u, e) if e < STEPS else (p, e - STEPS)
        rows = pl.ds(PAD + b * span, span)
        layer, landing = (depth, 0) if to_right else (1, depth + 1)
        way = 1 if to_right else 0
        to = jnp.minimum(me + 1, n - 1) if to_right else jnp.maximum(me - 1, 0)
        source = field.at[k, layer, rows, :]
        if e == 0:
            source = cur_hbm.at[layer - 1, pl.ds(b * span, span), :]
        return pltpu.make_async_remote_copy(
            src_ref=source, dst_ref=field.at[k, landing, rows, :],
            send_sem=send_sem.at[e, way, b], recv_sem=recv_sem.at[e, way, b],
            device_id={"gx": to}, device_id_type=MESH,
        )

    def send(e, to_right, b):
        @pl.when(has_right if to_right else has_left)
        def _():
            exchange(e, to_right, b).start()

    def receive(e, from_left, b):
        @pl.when(has_left if from_left else has_right)
        def _():
            exchange(e, from_left, b).wait_recv()

    def sent(e):
        for to_right, there in ((False, has_left), (True, has_right)):
            @pl.when(there)
            def _(to_right=to_right):
                for b in range(BLOCKS):
                    exchange(e, to_right, b).wait_send()

    for b in range(BLOCKS):
        send(0, False, b)
        send(0, True, b)

    border = jnp.zeros((PAD, side), jnp.float32)
    for field in (u, p):
        for k in range(STEPS):
            def clear(x, carry, field=field, k=k):
                field[k, x, 0:PAD, :] = border
                field[k, x, PAD + side : PAD + side + PAD, :] = border
                return carry

            lax.fori_loop(0, depth + 2, clear, 0)

    def clear_halo(layer):
        for field in (u, p):
            for k in range(STEPS):
                field[k, layer, PAD : PAD + side, :] = jnp.zeros((side, side), jnp.float32)

    @pl.when(me == 0)
    def _():
        clear_halo(0)

    @pl.when(me == n - 1)
    def _():
        clear_halo(depth + 1)

    lane = lax.broadcasted_iota(jnp.int32, (ROWS, side), 1)
    row = lax.broadcasted_iota(jnp.int32, (ROWS, side), 0)

    for x in range(depth):
        for f in range(4):
            map_t[f, x : x + 1, :] = map_ref[x, f : f + 1, :]
    maps = [map_t[f] for f in range(4)]

    def look_up(i, found):
        value = absorb_ref[i]
        return tuple(jnp.where(m == i, value, s) for m, s in zip(maps, found))

    found = lax.fori_loop(
        0, patches, look_up, tuple(jnp.zeros((depth, side), jnp.float32) for _ in range(4)),
        unroll=4,
    )
    for f in range(4):
        faces[f] = found[f]

    def spread(x, carry):
        f0, f1, f2, f3 = (faces[f, pl.ds(x, 1), :] for f in range(4))
        for r in range(0, side, ROWS):
            diagonal = lane == row + r
            c2 = jnp.sum(jnp.where(diagonal, f2, 0.0), axis=1, keepdims=True)
            c3 = jnp.sum(jnp.where(diagonal, f3, 0.0), axis=1, keepdims=True)
            s = jnp.where(lane == 0, c2, 0.0) + jnp.where(lane == side - 1, c3, 0.0)
            if r == 0:
                s = s + jnp.where(row == 0, f0, 0.0)
            if r == side - ROWS:
                s = s + jnp.where(row == ROWS - 1, f1, 0.0)
            damp[x, r : r + ROWS, :] = s
            inv[x, r : r + ROWS, :] = 1.0 / (1.0 + s)
        return carry

    lax.fori_loop(0, depth, spread, 0)
    for copy in loads:
        copy.wait()

    def around(field, k, x, r):
        tall = field[k, x + 1, pl.ds(r, ROWS + 2 * PAD), :]
        mid = tall[PAD : PAD + ROWS]
        here = pl.ds(r + PAD, ROWS)
        total = field[k, x, here, :] + field[k, x + 2, here, :]
        total = total + tall[PAD - 1 : PAD - 1 + ROWS] + tall[PAD + 1 : PAD + 1 + ROWS]
        total = total + jnp.where(lane == 0, 0.0, pltpu.roll(mid, 1, 1))
        total = total + jnp.where(lane == side - 1, 0.0, pltpu.roll(mid, side - 1, 1))
        return mid, total

    def middle(body, carry):
        def step(x, carry):
            for r in range(0, side, ROWS):
                carry = body(x, r, carry)
            return carry

        return lax.fori_loop(1, depth - 1, step, carry)

    def outer(e, body, carry, last_one=False):
        for b in range(BLOCKS):
            for x, is_right in ((0, False), (depth - 1, True)):
                receive(e, not is_right, b)
                for r in range(b * span, (b + 1) * span, ROWS):
                    carry = body(x, r, carry)
                if not last_one:
                    send(e + 1, is_right, b)
        return carry

    def forward(k):
        def body(x, r, acc):
            at = pl.ds(r, ROWS)
            here = pl.ds(r + PAD, ROWS)
            mid, total = around(u, k, x, r)
            prior = prev[x, at, :] if k == 0 else u[k - 1, x + 1, here, :]
            c = cs[x, at, :]
            scale = inv[x, at, :]
            new = (2.0 * mid - (1.0 - damp[x, at, :]) * prior + c * (total - 6.0 * mid)) * scale
            if k < STEPS - 1:
                u[k + 1, x + 1, here, :] = new
            else:
                last[x, at, :] = new
                weighted = scale * new
                w[STEPS - 1, x, at, :] = weighted
                p[0, x + 1, here, :] = c * weighted
            square = new * new
            for b in range(0, ROWS, 8):
                acc = acc + square[b : b + 8]
            return acc

        return body

    nothing = jnp.zeros((8, side), jnp.float32)
    for k in range(STEPS):
        acc = outer(k, forward(k), nothing)
        energy[k] = middle(forward(k), acc)

    emsg[...] = jnp.zeros_like(emsg)
    for k in range(STEPS):
        line = jnp.sum(energy[k], axis=0, keepdims=True)
        half = line[:, :128]
        for b in range(128, side, 128):
            half = half + line[:, b : b + 128]
        emsg[k : k + 1, :] = half

    def e_copy(d):
        return pltpu.make_async_remote_copy(
            src_ref=emsg, dst_ref=eslots.at[d], send_sem=esend.at[d], recv_sem=erecv.at[d],
            device_id={"gx": lax.rem(me + d, n)}, device_id_type=MESH,
        )

    def p_copy(d):
        to = lax.rem(me + d, n)
        return pltpu.make_async_remote_copy(
            src_ref=part.at[to], dst_ref=pslots.at[d], send_sem=psend.at[d], recv_sem=precv.at[d],
            device_id={"gx": to}, device_id_type=MESH,
        )

    def each(action):
        def step(d, carry):
            action(d)
            return carry

        lax.fori_loop(1, n, step, 0)

    each(lambda d: e_copy(d).start())
    each(lambda d: e_copy(d).wait_recv())
    summed = lax.fori_loop(1, n, lambda d, t: t + eslots[d], emsg[...])
    summed = jnp.sum(summed, axis=1, keepdims=True) / all_cells
    tail, start = tail_ref[0], check_ref[0]
    later = jnp.zeros((1, side), jnp.float32) + tail
    slopes = [None] * STEPS
    for k in range(STEPS - 1, -1, -1):
        later = later + summed[k : k + 1, :]
        slopes[k] = 2.0 * (jnp.log(later) - target_ref[start + k]) / later
    running = jnp.zeros((1, side), jnp.float32)
    for k in range(STEPS):
        running = running + slopes[k]
        gains[k : k + 1, :] = 2.0 * running

    def backward(j):
        slot = STEPS - j

        def body(x, r, carry):
            at = pl.ds(r, ROWS)
            here = pl.ds(r + PAD, ROWS)
            mid, total = around(p, slot, x, r)
            fresh = 2.0 * w[j - 1, x, at, :] + total - 6.0 * mid
            if j == STEPS:
                fresh = fresh * gains[STEPS - 1 : STEPS, :]
            else:
                after = w[j, x, at, :]
                if j == STEPS - 1:
                    after = after * gains[STEPS - 1 : STEPS, :]
                fresh = fresh - (1.0 - damp[x, at, :]) * after
            if j == 1:
                gcur[x, at, :] = fresh
                return carry
            fresh = fresh + gains[j - 2 : j - 1, :] * u[j - 1, x + 1, here, :]
            weighted = inv[x, at, :] * fresh
            w[j - 2, x, at, :] = weighted
            p[slot + 1, x + 1, here, :] = cs[x, at, :] * weighted
            if j == 2:
                gprev[x, at, :] = (damp[x, at, :] - 1.0) * weighted
            return carry

        return body

    def state(k, x, at, cells):
        if k < 0:
            return prev[x, at, cells]
        if k == STEPS:
            return last[x, at, cells]
        return u[k, x + 1, pl.ds(at.start + PAD, at.size), cells]

    def product(steps, x, at, cells):
        total = None
        for j in steps:
            term = w[j - 1, x, at, cells] * (state(j - 2, x, at, cells) - state(j, x, at, cells))
            if j == STEPS:
                term = term * gains[STEPS - 1 : STEPS, cells]
            total = term if total is None else total + term
        return total

    def collect(steps, x, carry):
        first = STEPS in steps

        def keep(f, line):
            faces[f, pl.ds(x, 1), :] = line if first else faces[f, pl.ds(x, 1), :] + line

        top = product(steps, x, pl.ds(0, 8), slice(0, side))
        bottom = product(steps, x, pl.ds(side - 8, 8), slice(0, side))
        keep(0, top[0:1])
        keep(1, bottom[7:8])

        lines = [jnp.zeros((1, side), jnp.float32)] * 2
        for r in range(0, side, ROWS):
            diagonal = lane == row + r
            at = pl.ds(r, ROWS)
            left = product(steps, x, at, slice(0, 128))[:, 0:1]
            right = product(steps, x, at, slice(side - 128, side))[:, 127:128]
            lines = [
                line + jnp.sum(jnp.where(diagonal, c, 0.0), axis=0, keepdims=True)
                for line, c in zip(lines, (left, right))
            ]
        keep(2, lines[0])
        keep(3, lines[1])
        return carry

    for j in range(STEPS, 1, -1):
        outer(2 * STEPS - j, backward(j), 0)
        middle(backward(j), 0)
        if j == 3:
            lax.fori_loop(0, depth, functools.partial(collect, (4, 3, 2)), 0)
    lax.fori_loop(0, depth, functools.partial(collect, (1,)), 0)

    place = lax.broadcasted_iota(jnp.int32, (8, 128), 1)

    walls = [faces[f] for f in range(4)]

    def by_owner(i, carry):
        tile = jnp.zeros((8, 128), jnp.float32)
        for k in range(owned):
            hit = None
            for f in range(4):
                term = jnp.where(maps[f] == i * owned + k, walls[f], 0.0)
                hit = term if hit is None else hit + term
            line = jnp.sum(hit, axis=0, keepdims=True)
            whole = jnp.sum(line, axis=1, keepdims=True)
            tile = jnp.where(place == k, whole, tile)
        part[i] = tile
        return carry

    lax.fori_loop(0, n, by_owner, 0)
    each(lambda d: p_copy(d).start())

    middle(backward(1), 0)
    outer(2 * STEPS - 1, backward(1), 0, last_one=True)

    each(lambda d: p_copy(d).wait_recv())
    mine = lax.fori_loop(1, n, lambda d, t: t + pslots[d], part[me])
    gabs_ref[...] = mine / float(PATCH_CELLS)

    for e in range(2 * STEPS):
        sent(e)
    each(lambda d: e_copy(d).wait_send())
    each(lambda d: p_copy(d).wait_send())


def on_device(n, u_prev, u_cur, courant_sq, patch_map, absorb, checkpoint, target_curve, tail_energy):
    depth, side = u_cur.shape[0], u_cur.shape[1]
    f32 = jnp.float32
    brick = pltpu.VMEM((depth, side, side), f32)
    padded = pltpu.VMEM((STEPS, depth + 2, side + 2 * PAD, side), f32)
    hbm = pl.BlockSpec(memory_space=pl.ANY)
    vmem = pl.BlockSpec(memory_space=pltpu.VMEM)
    smem = pl.BlockSpec(memory_space=pltpu.SMEM)
    dma = pltpu.SemaphoreType.DMA
    grad_prev, grad_cur, tile = pl.pallas_call(
        functools.partial(kernel, n, float(depth * n * side * side)),
        out_shape=(
            pltpu.VMEM(u_cur.shape, f32),
            pltpu.VMEM(u_cur.shape, f32),
            jax.ShapeDtypeStruct((8, 128), f32),
        ),
        in_specs=[hbm, hbm, hbm, vmem, smem, smem, smem, smem],
        out_specs=(vmem, vmem, vmem),
        scratch_shapes=[
            padded, padded, brick, brick, brick, brick, brick,
            pltpu.VMEM((STEPS, depth, side, side), f32),
            pltpu.VMEM((4, depth, side), jnp.int32),
            pltpu.VMEM((4, depth, side), f32),
            pltpu.VMEM((STEPS, 8, side), f32),
            pltpu.VMEM((8, 128), f32),
            pltpu.VMEM((n, 8, 128), f32),
            pltpu.VMEM((8, side), f32),
            pltpu.VMEM((n, 8, 128), f32),
            pltpu.VMEM((n, 8, 128), f32),
            dma((7,)), dma((2 * STEPS, 2, BLOCKS)), dma((2 * STEPS, 2, BLOCKS)),
            dma((n,)), dma((n,)), dma((n,)), dma((n,)),
        ],
        compiler_params=pltpu.CompilerParams(
            collective_id=0, has_side_effects=True, vmem_limit_bytes=56 * 1024 * 1024
        ),
    )(u_prev, u_cur, courant_sq, patch_map, absorb, checkpoint, target_curve, tail_energy)
    return grad_prev, grad_cur, tile[0, : absorb.shape[0] // n]


def solution(mesh):
    field = P(("groups", "gx"), None, None)
    return jax.shard_map(
        functools.partial(on_device, mesh.shape["gx"]),
        mesh=mesh,
        in_specs=(field, field, field, field, P("groups"), P("groups"), P("groups"), P("groups")),
        out_specs=(field, field, P(("groups", "gx"))),
        check_vma=False,
    )
```

```python
import functools

import jax
import jax.numpy as jnp
from jax import lax
from jax.experimental import pallas as pl
from jax.experimental.pallas import tpu as pltpu
from jax.sharding import PartitionSpec as P

STEPS = 4
PATCH_CELLS = 819
PAD = 8
ROWS = 32
BLOCKS = 2
MESH = pl.DeviceIdType.MESH


def kernel(
    n, all_cells,
    prev_hbm, cur_hbm, courant_hbm, map_ref, absorb_ref, check_ref, target_ref, tail_ref,
    gprev, gcur, gabs_ref,
    u, p, last, prev, cs, damp, inv, w,
    map_t, faces, energy, emsg, eslots, gains, part, pslots,
    local_sem, send_sem, recv_sem, esend, erecv, psend, precv,
):
    me = lax.axis_index("gx")
    depth, side = prev.shape[0], prev.shape[1]
    patches = absorb_ref.shape[0]
    owned = patches // n
    inner = pl.ds(PAD, side)
    has_left, has_right = me > 0, me < n - 1

    loads = [
        pltpu.make_async_copy(cur_hbm, u.at[0, pl.ds(1, depth), inner, :], local_sem.at[0]),
        pltpu.make_async_copy(prev_hbm, prev, local_sem.at[1]),
        pltpu.make_async_copy(courant_hbm, cs, local_sem.at[2]),
    ]
    for copy in loads:
        copy.start()

    barrier = pltpu.get_barrier_semaphore()

    def greet(d, carry):
        pl.semaphore_signal(
            barrier, inc=1, device_id={"gx": lax.rem(me + d, n)}, device_id_type=MESH
        )
        return carry

    lax.fori_loop(1, n, greet, 0)
    pl.semaphore_wait(barrier, n - 1)

    span = side // BLOCKS

    def exchange(e, to_right, b):
        field, k = (u, e) if e < STEPS else (p, e - STEPS)
        rows = pl.ds(PAD + b * span, span)
        layer, landing = (depth, 0) if to_right else (1, depth + 1)
        way = 1 if to_right else 0
        to = jnp.minimum(me + 1, n - 1) if to_right else jnp.maximum(me - 1, 0)
        source = field.at[k, layer, rows, :]
        if e == 0:
            source = cur_hbm.at[layer - 1, pl.ds(b * span, span), :]
        return pltpu.make_async_remote_copy(
            src_ref=source, dst_ref=field.at[k, landing, rows, :],
            send_sem=send_sem.at[e, way, b], recv_sem=recv_sem.at[e, way, b],
            device_id={"gx": to}, device_id_type=MESH,
        )

    def send(e, to_right, b):
        @pl.when(has_right if to_right else has_left)
        def _():
            exchange(e, to_right, b).start()

    def receive(e, from_left, b):
        @pl.when(has_left if from_left else has_right)
        def _():
            exchange(e, from_left, b).wait_recv()

    def sent(e):
        for to_right, there in ((False, has_left), (True, has_right)):
            @pl.when(there)
            def _(to_right=to_right):
                for b in range(BLOCKS):
                    exchange(e, to_right, b).wait_send()

    for b in range(BLOCKS):
        send(0, False, b)
        send(0, True, b)

    border = jnp.zeros((PAD, side), jnp.float32)
    for field in (u, p):
        for k in range(STEPS):
            def clear(x, carry, field=field, k=k):
                field[k, x, 0:PAD, :] = border
                field[k, x, PAD + side : PAD + side + PAD, :] = border
                return carry

            lax.fori_loop(0, depth + 2, clear, 0)

    def clear_halo(layer):
        for field in (u, p):
            for k in range(STEPS):
                field[k, layer, PAD : PAD + side, :] = jnp.zeros((side, side), jnp.float32)

    @pl.when(me == 0)
    def _():
        clear_halo(0)

    @pl.when(me == n - 1)
    def _():
        clear_halo(depth + 1)

    lane = lax.broadcasted_iota(jnp.int32, (ROWS, side), 1)
    row = lax.broadcasted_iota(jnp.int32, (ROWS, side), 0)

    for x in range(depth):
        for f in range(4):
            map_t[f, x : x + 1, :] = map_ref[x, f : f + 1, :]
    maps = [map_t[f] for f in range(4)]

    def look_up(i, found):
        value = absorb_ref[i]
        return tuple(jnp.where(m == i, value, s) for m, s in zip(maps, found))

    found = lax.fori_loop(
        0, patches, look_up, tuple(jnp.zeros((depth, side), jnp.float32) for _ in range(4)),
        unroll=4,
    )
    for f in range(4):
        faces[f] = found[f]

    def spread(x, carry):
        f0, f1, f2, f3 = (faces[f, pl.ds(x, 1), :] for f in range(4))
        for r in range(0, side, ROWS):
            diagonal = lane == row + r
            c2 = jnp.sum(jnp.where(diagonal, f2, 0.0), axis=1, keepdims=True)
            c3 = jnp.sum(jnp.where(diagonal, f3, 0.0), axis=1, keepdims=True)
            s = jnp.where(lane == 0, c2, 0.0) + jnp.where(lane == side - 1, c3, 0.0)
            if r == 0:
                s = s + jnp.where(row == 0, f0, 0.0)
            if r == side - ROWS:
                s = s + jnp.where(row == ROWS - 1, f1, 0.0)
            damp[x, r : r + ROWS, :] = s
            inv[x, r : r + ROWS, :] = 1.0 / (1.0 + s)
        return carry

    lax.fori_loop(0, depth, spread, 0)
    for copy in loads:
        copy.wait()

    def around(field, k, x, r):
        tall = field[k, x + 1, pl.ds(r, ROWS + 2 * PAD), :]
        mid = tall[PAD : PAD + ROWS]
        here = pl.ds(r + PAD, ROWS)
        total = field[k, x, here, :] + field[k, x + 2, here, :]
        total = total + tall[PAD - 1 : PAD - 1 + ROWS] + tall[PAD + 1 : PAD + 1 + ROWS]
        total = total + jnp.where(lane == 0, 0.0, pltpu.roll(mid, 1, 1))
        total = total + jnp.where(lane == side - 1, 0.0, pltpu.roll(mid, side - 1, 1))
        return mid, total

    def middle(body, carry):
        def step(x, carry):
            for r in range(0, side, ROWS):
                carry = body(x, r, carry)
            return carry

        return lax.fori_loop(1, depth - 1, step, carry)

    def outer(e, body, carry, last_one=False):
        for b in range(BLOCKS):
            for x, is_right in ((0, False), (depth - 1, True)):
                receive(e, not is_right, b)
                for r in range(b * span, (b + 1) * span, ROWS):
                    carry = body(x, r, carry)
                if not last_one:
                    send(e + 1, is_right, b)
        return carry

    def forward(k):
        def body(x, r, acc):
            at = pl.ds(r, ROWS)
            here = pl.ds(r + PAD, ROWS)
            mid, total = around(u, k, x, r)
            prior = prev[x, at, :] if k == 0 else u[k - 1, x + 1, here, :]
            c = cs[x, at, :]
            scale = inv[x, at, :]
            new = (2.0 * mid - (1.0 - damp[x, at, :]) * prior + c * (total - 6.0 * mid)) * scale
            if k < STEPS - 1:
                u[k + 1, x + 1, here, :] = new
            else:
                last[x, at, :] = new
                weighted = scale * new
                w[STEPS - 1, x, at, :] = weighted
                p[0, x + 1, here, :] = c * weighted
            square = new * new
            for b in range(0, ROWS, 8):
                acc = acc + square[b : b + 8]
            return acc

        return body

    nothing = jnp.zeros((8, side), jnp.float32)
    for k in range(STEPS):
        if k == STEPS - 1:
            energy[k] = outer(k, forward(k), middle(forward(k), nothing))
        else:
            energy[k] = middle(forward(k), outer(k, forward(k), nothing))

    emsg[...] = jnp.zeros_like(emsg)
    for k in range(STEPS):
        line = jnp.sum(energy[k], axis=0, keepdims=True)
        half = line[:, :128]
        for b in range(128, side, 128):
            half = half + line[:, b : b + 128]
        emsg[k : k + 1, :] = half

    def e_copy(d):
        return pltpu.make_async_remote_copy(
            src_ref=emsg, dst_ref=eslots.at[d], send_sem=esend.at[d], recv_sem=erecv.at[d],
            device_id={"gx": lax.rem(me + d, n)}, device_id_type=MESH,
        )

    def p_copy(d):
        to = lax.rem(me + d, n)
        return pltpu.make_async_remote_copy(
            src_ref=part.at[to], dst_ref=pslots.at[d], send_sem=psend.at[d], recv_sem=precv.at[d],
            device_id={"gx": to}, device_id_type=MESH,
        )

    def each(action):
        def step(d, carry):
            action(d)
            return carry

        lax.fori_loop(1, n, step, 0)

    each(lambda d: e_copy(d).start())
    each(lambda d: e_copy(d).wait_recv())
    summed = lax.fori_loop(1, n, lambda d, t: t + eslots[d], emsg[...])
    summed = jnp.sum(summed, axis=1, keepdims=True) / all_cells
    tail, start = tail_ref[0], check_ref[0]
    later = jnp.zeros((1, side), jnp.float32) + tail
    slopes = [None] * STEPS
    for k in range(STEPS - 1, -1, -1):
        later = later + summed[k : k + 1, :]
        slopes[k] = 2.0 * (jnp.log(later) - target_ref[start + k]) / later
    running = jnp.zeros((1, side), jnp.float32)
    for k in range(STEPS):
        running = running + slopes[k]
        gains[k : k + 1, :] = 2.0 * running

    def backward(j):
        slot = STEPS - j

        def body(x, r, carry):
            at = pl.ds(r, ROWS)
            here = pl.ds(r + PAD, ROWS)
            mid, total = around(p, slot, x, r)
            fresh = 2.0 * w[j - 1, x, at, :] + total - 6.0 * mid
            if j == STEPS:
                fresh = fresh * gains[STEPS - 1 : STEPS, :]
            else:
                after = w[j, x, at, :]
                if j == STEPS - 1:
                    after = after * gains[STEPS - 1 : STEPS, :]
                fresh = fresh - (1.0 - damp[x, at, :]) * after
            if j == 1:
                gcur[x, at, :] = fresh
                return carry
            fresh = fresh + gains[j - 2 : j - 1, :] * u[j - 1, x + 1, here, :]
            weighted = inv[x, at, :] * fresh
            w[j - 2, x, at, :] = weighted
            p[slot + 1, x + 1, here, :] = cs[x, at, :] * weighted
            if j == 2:
                gprev[x, at, :] = (damp[x, at, :] - 1.0) * weighted
            return carry

        return body

    def state(k, x, at, cells):
        if k < 0:
            return prev[x, at, cells]
        if k == STEPS:
            return last[x, at, cells]
        return u[k, x + 1, pl.ds(at.start + PAD, at.size), cells]

    def product(steps, x, at, cells):
        total = None
        for j in steps:
            term = w[j - 1, x, at, cells] * (state(j - 2, x, at, cells) - state(j, x, at, cells))
            if j == STEPS:
                term = term * gains[STEPS - 1 : STEPS, cells]
            total = term if total is None else total + term
        return total

    def collect(steps, x, carry):
        first = STEPS in steps

        def keep(f, line):
            faces[f, pl.ds(x, 1), :] = line if first else faces[f, pl.ds(x, 1), :] + line

        top = product(steps, x, pl.ds(0, 8), slice(0, side))
        bottom = product(steps, x, pl.ds(side - 8, 8), slice(0, side))
        keep(0, top[0:1])
        keep(1, bottom[7:8])

        lines = [jnp.zeros((1, side), jnp.float32)] * 2
        for r in range(0, side, ROWS):
            diagonal = lane == row + r
            at = pl.ds(r, ROWS)
            left = product(steps, x, at, slice(0, 128))[:, 0:1]
            right = product(steps, x, at, slice(side - 128, side))[:, 127:128]
            lines = [
                line + jnp.sum(jnp.where(diagonal, c, 0.0), axis=0, keepdims=True)
                for line, c in zip(lines, (left, right))
            ]
        keep(2, lines[0])
        keep(3, lines[1])
        return carry

    for j in range(STEPS, 1, -1):
        outer(2 * STEPS - j, backward(j), 0)
        middle(backward(j), 0)
        if j == 3:
            lax.fori_loop(0, depth, functools.partial(collect, (4, 3, 2)), 0)
    lax.fori_loop(0, depth, functools.partial(collect, (1,)), 0)

    place = lax.broadcasted_iota(jnp.int32, (8, 128), 1)

    walls = [faces[f] for f in range(4)]

    def by_owner(i, carry):
        tile = jnp.zeros((8, 128), jnp.float32)
        for k in range(owned):
            hit = None
            for f in range(4):
                term = jnp.where(maps[f] == i * owned + k, walls[f], 0.0)
                hit = term if hit is None else hit + term
            line = jnp.sum(hit, axis=0, keepdims=True)
            whole = jnp.sum(line, axis=1, keepdims=True)
            tile = jnp.where(place == k, whole, tile)
        part[i] = tile
        return carry

    lax.fori_loop(0, n, by_owner, 0)
    each(lambda d: p_copy(d).start())

    middle(backward(1), 0)
    outer(2 * STEPS - 1, backward(1), 0, last_one=True)

    each(lambda d: p_copy(d).wait_recv())
    mine = lax.fori_loop(1, n, lambda d, t: t + pslots[d], part[me])
    gabs_ref[...] = mine / float(PATCH_CELLS)

    for e in range(2 * STEPS):
        sent(e)
    each(lambda d: e_copy(d).wait_send())
    each(lambda d: p_copy(d).wait_send())


def on_device(n, u_prev, u_cur, courant_sq, patch_map, absorb, checkpoint, target_curve, tail_energy):
    depth, side = u_cur.shape[0], u_cur.shape[1]
    f32 = jnp.float32
    brick = pltpu.VMEM((depth, side, side), f32)
    padded = pltpu.VMEM((STEPS, depth + 2, side + 2 * PAD, side), f32)
    hbm = pl.BlockSpec(memory_space=pl.ANY)
    vmem = pl.BlockSpec(memory_space=pltpu.VMEM)
    smem = pl.BlockSpec(memory_space=pltpu.SMEM)
    dma = pltpu.SemaphoreType.DMA
    grad_prev, grad_cur, tile = pl.pallas_call(
        functools.partial(kernel, n, float(depth * n * side * side)),
        out_shape=(
            pltpu.VMEM(u_cur.shape, f32),
            pltpu.VMEM(u_cur.shape, f32),
            jax.ShapeDtypeStruct((8, 128), f32),
        ),
        in_specs=[hbm, hbm, hbm, vmem, smem, smem, smem, smem],
        out_specs=(vmem, vmem, vmem),
        scratch_shapes=[
            padded, padded, brick, brick, brick, brick, brick,
            pltpu.VMEM((STEPS, depth, side, side), f32),
            pltpu.VMEM((4, depth, side), jnp.int32),
            pltpu.VMEM((4, depth, side), f32),
            pltpu.VMEM((STEPS, 8, side), f32),
            pltpu.VMEM((8, 128), f32),
            pltpu.VMEM((n, 8, 128), f32),
            pltpu.VMEM((8, side), f32),
            pltpu.VMEM((n, 8, 128), f32),
            pltpu.VMEM((n, 8, 128), f32),
            dma((7,)), dma((2 * STEPS, 2, BLOCKS)), dma((2 * STEPS, 2, BLOCKS)),
            dma((n,)), dma((n,)), dma((n,)), dma((n,)),
        ],
        compiler_params=pltpu.CompilerParams(
            collective_id=0, has_side_effects=True, vmem_limit_bytes=56 * 1024 * 1024
        ),
    )(u_prev, u_cur, courant_sq, patch_map, absorb, checkpoint, target_curve, tail_energy)
    return grad_prev, grad_cur, tile[0, : absorb.shape[0] // n]


def solution(mesh):
    field = P(("groups", "gx"), None, None)
    return jax.shard_map(
        functools.partial(on_device, mesh.shape["gx"]),
        mesh=mesh,
        in_specs=(field, field, field, field, P("groups"), P("groups"), P("groups"), P("groups")),
        out_specs=(field, field, P(("groups", "gx"))),
        check_vma=False,
    )
```
